512 devices in a mesh: section: 16 (over y, z_hi), tp: 32 (over z_lo, x, core).
Axes of the slice: x: 4, y: 4, z: 16 (z_hi: 4, z_lo: 4; z = z_hi * 4 + z_lo), core: 2. Of those that a mesh axis runs over, the one named last changes fastest.
Arguments:
- grad_in: bfloat16 [16, 128, 4096], P('section', None, 'tp'), may hold values from -6 to 6
- fresh_grads: bfloat16 [1, 128, 4096], P(None, None, 'tp'), may hold values from -6 to 6
- acc_in: float32 [16, 128, 4096], P('section', None, 'tp'), may hold values from -3 to 3
- queries: bfloat16 [16, 2, 128, 4096], P('section', None, None, 'tp'), may hold values from -4.625 to 4.625
- keys: bfloat16 [16, 2, 128, 4096], P('section', None, None, 'tp'), may hold values from -4.625 to 4.625
- values: bfloat16 [16, 2, 128, 4096], P('section', None, None, 'tp'), may hold values from -12 to 12
- query_weight: bfloat16 [16, 4096, 4096], P('section', 'tp'), may hold values from -0.09375 to 0.09375
- key_weight: bfloat16 [16, 4096, 4096], P('section', None, 'tp'), may hold values from -0.1875 to 0.1875
- value_weight: bfloat16 [16, 4096, 4096], P('section', None, 'tp'), may hold values from -0.1875 to 0.1875
- out_weight: bfloat16 [16, 4096, 4096], P('section', 'tp'), may hold values from -0.09375 to 0.09375
Outputs:
- grad_out: bfloat16 [16, 128, 4096], P('section', None, 'tp')
- acc_out: float32 [16, 128, 4096], P('section', None, 'tp')
The draws below stay inside these ranges and needn't reach their ends.
All inputs are finite; a program needn't handle non-finite values.
Results may differ from the reference program's by a relative error of at most 0.025.
Values may be sent and summed in bfloat16 or wider, within the bound.
No kernel may reach another device: no remote copies, remote signals or barrier semaphores. Data moves between devices by JAX's collectives and lax.ppermute only.
A program may use at most 64 MiB of HBM per device.

```python
import jax
import jax.numpy as jnp
from jax import lax

D = 4096
HEADS = 64
HEAD_DIM = 64
SEQS = 1
DEC_LEN = 128
ENC_LEN = 128
MICRO = 2
SECTIONS = 16
INNER = 4096
TOK = 128
ENC_ROWS = 128
N_TP = 32


def draw_queries(key, part):
    noise_key = jax.random.fold_in(key, 1)
    full_shape = (SECTIONS, MICRO, SEQS, DEC_LEN, HEADS, HEAD_DIM)
    field = jnp.clip(0.35 * jax.random.normal(noise_key, full_shape, jnp.float32), -2.5, 2.5)
    return field.reshape(SECTIONS, MICRO, SEQS * DEC_LEN, HEADS * HEAD_DIM).astype(jnp.bfloat16)


def draw_keys(key, part):
    noise_key = jax.random.fold_in(key, 2)
    full_shape = (SECTIONS, MICRO, SEQS, ENC_LEN, HEADS, HEAD_DIM)
    field = jnp.clip(0.5 * jax.random.normal(noise_key, full_shape, jnp.float32), -2.5, 2.5)
    return field.reshape(SECTIONS, MICRO, SEQS * ENC_LEN, HEADS * HEAD_DIM).astype(jnp.bfloat16)


def raised(entries, rng, source, target, parts, factor):
    owner, partner = [(jnp.arange(entries.shape[dim]) // (entries.shape[dim] // parts)).reshape([-1 if axis == dim else 1 for axis in range(entries.ndim)]) for dim in (source, target)]
    chosen = jax.random.permutation(rng, parts)[partner]
    strong = (owner == chosen) | (owner == (partner + parts // 2) % parts)
    return jnp.where(strong, factor * entries, entries)


def block_scale(own_key, dims, cuts, least, largest):
    def one(position, shards_of):
        steps = jax.random.uniform(jax.random.fold_in(jax.random.fold_in(own_key, 6), position), (shards_of,), jnp.float32, least / len(cuts), largest / len(cuts))
        return jnp.repeat(jnp.exp(steps), dims[position] // shards_of).reshape((-1,) + (1,) * (len(dims) - position - 1))

    loudness = one(*cuts[0])
    for cut in cuts[1:]:
        loudness = loudness * one(*cut)
    return loudness


def centred(rng, dims, spread, reach, pieces=(), held_as=jnp.bfloat16):
    result = spread * jax.random.normal(rng, dims, jnp.float32)
    if pieces:
        result = result * block_scale(rng, dims, pieces, -0.22, 0.18)
    return jnp.clip(result, -reach, reach).astype(held_as)


def noise_with(key, shape, deviation, most, pieces, heavy, kind=jnp.bfloat16):
    values = deviation * jax.random.normal(key, shape, jnp.float32)
    if pieces:
        values = values * block_scale(key, shape, pieces, -0.22, 0.18)
    return jnp.clip(raised(values, jax.random.fold_in(key, 3), *heavy), -most, most).astype(kind)


def setup_inputs(seed: int = 0) -> dict:
    splits = jax.random.split(jax.random.key(seed), 11)
    return {
        "grad_in": centred(splits[0], (SECTIONS, TOK, D), 1.0, 6.0, ((0, 16), (2, 32))),
        "fresh_grads": centred(splits[1], (MICRO - 1, TOK, D), 1.0, 6.0, ((2, 32),)),
        "acc_in": centred(splits[2], (SECTIONS, ENC_ROWS, D), 0.5, 3.0, ((0, 16), (2, 32)), jnp.float32),
        "queries": draw_queries(jax.random.fold_in(splits[10], 71), 0),
        "keys": draw_keys(jax.random.fold_in(splits[10], 71), 0),
        "values": centred(splits[5], (SECTIONS, MICRO, ENC_ROWS, INNER), 2.0, 12.0, ((0, 16), (3, 32))),
        "query_weight": centred(splits[6], (SECTIONS, D, INNER), D ** -0.5, 0.09375, ((0, 16), (1, 32))),
        "key_weight": noise_with(splits[7], (SECTIONS, D, INNER), D ** -0.5, 0.1875, ((0, 16), (2, 32)), (2, 1, 32, 2.75)),
        "value_weight": noise_with(splits[8], (SECTIONS, D, INNER), D ** -0.5, 0.1875, ((0, 16), (2, 32)), (2, 1, 32, 2.75)),
        "out_weight": centred(splits[9], (SECTIONS, INNER, D), INNER ** -0.5, 0.09375, ((0, 16), (1, 32))),
    }


def attention_grads(upstream, queries, keys, values):
    token_rows, columns = queries.shape
    enc_rows = keys.shape[0]
    query_heads = queries.astype(jnp.float32).reshape(SEQS, token_rows // SEQS, HEADS, HEAD_DIM)
    key_heads = keys.astype(jnp.float32).reshape(SEQS, enc_rows // SEQS, HEADS, HEAD_DIM)
    value_heads = values.astype(jnp.float32).reshape(SEQS, enc_rows // SEQS, HEADS, HEAD_DIM)
    upstream_heads = upstream.astype(jnp.float32).reshape(SEQS, token_rows // SEQS, HEADS, HEAD_DIM)
    scores = jnp.einsum("bqhd,bkhd->bhqk", query_heads, key_heads, precision=lax.Precision.HIGHEST)
    attention = jax.nn.softmax(scores, axis=-1)
    weights = attention.astype(jnp.bfloat16).astype(jnp.float32)
    output = jnp.einsum("bhqk,bkhd->bqhd", weights, value_heads, precision=lax.Precision.HIGHEST)
    delta = jnp.sum(upstream_heads * output, axis=-1)
    prob_grad = jnp.einsum("bqhd,bkhd->bhqk", upstream_heads, value_heads, precision=lax.Precision.HIGHEST)
    score_grad = (attention * (prob_grad - jnp.transpose(delta, (0, 2, 1))[..., None])).astype(jnp.bfloat16)
    score_grad = score_grad.astype(jnp.float32)
    query_grad = jnp.einsum("bhqk,bkhd->bqhd", score_grad, key_heads, precision=lax.Precision.HIGHEST)
    key_grad = jnp.einsum("bhqk,bqhd->bkhd", score_grad, query_heads, precision=lax.Precision.HIGHEST)
    value_grad = jnp.einsum("bhqk,bqhd->bkhd", weights, upstream_heads, precision=lax.Precision.HIGHEST)
    return (query_grad.reshape(token_rows, columns).astype(jnp.bfloat16),
            key_grad.reshape(enc_rows, columns).astype(jnp.bfloat16),
            value_grad.reshape(enc_rows, columns).astype(jnp.bfloat16))


def section_step(inputs):
    grad, carried, query_rows, key_rows, value_rows, w_query, w_key, w_value, w_out = inputs
    upstream = jnp.dot(grad, w_out.T, preferred_element_type=jnp.float32).astype(jnp.bfloat16)
    query_grad, key_grad, value_grad = attention_grads(upstream, query_rows, key_rows, value_rows)
    branch = jnp.dot(query_grad, w_query.T, preferred_element_type=jnp.float32)
    passed = (grad.astype(jnp.float32) + branch).astype(jnp.bfloat16)
    group_width = w_key.shape[1] // N_TP
    enc_rows = key_grad.shape[0]
    key_groups = key_grad.astype(jnp.float32).reshape(enc_rows, N_TP, group_width)
    value_groups = value_grad.astype(jnp.float32).reshape(enc_rows, N_TP, group_width)
    key_cols = w_key.astype(jnp.float32).reshape(w_key.shape[0], N_TP, group_width)
    value_cols = w_value.astype(jnp.float32).reshape(w_value.shape[0], N_TP, group_width)
    terms = jnp.einsum("rgc,dgc->grd", key_groups, key_cols, precision=lax.Precision.HIGHEST)
    terms = terms + jnp.einsum("rgc,dgc->grd", value_groups, value_cols, precision=lax.Precision.HIGHEST)
    rounded = lax.optimization_barrier(terms.astype(jnp.bfloat16)).astype(jnp.float32)
    return passed, carried + jnp.sum(rounded, axis=0)


def reference(grad_in, fresh_grads, acc_in, queries, keys, values, query_weight, key_weight, value_weight, out_weight):
    grads = grad_in
    sums = acc_in
    passed = grad_in
    updated = acc_in
    for slot in range(MICRO):
        passed, updated = lax.map(section_step, (grads, sums, queries[:, slot], keys[:, slot], values[:, slot],
                                               query_weight, key_weight, value_weight, out_weight))
        if slot + 1 < MICRO:
            grads = jnp.concatenate([passed[1:], fresh_grads[slot][None]], axis=0)
            sums = jnp.concatenate([updated[1:], jnp.zeros_like(updated[:1])], axis=0)
    return passed, updated
```

```python
import jax
import jax.numpy as jnp
from jax import lax
from jax.sharding import PartitionSpec as P

HEAD_DIM = 64
CORES = 2


def passed_along(value, axis, steps):
    count = lax.axis_size(axis)
    leading, last = (max(0, -steps), min(count, count - steps))
    return lax.ppermute(value, axis, [(source, source + steps) for source in range(leading, last)])


def chip_groups():
    chips = lax.axis_size("tp") // CORES
    return [[chip * CORES + core for chip in range(chips)] for core in range(CORES)]


def core_groups():
    chips = lax.axis_size("tp") // CORES
    return [[chip * CORES + core for core in range(CORES)] for chip in range(chips)]


def chip_exchange(parts):
    return lax.all_to_all(
        parts, "tp", split_axis=0, concat_axis=0, tiled=True, axis_index_groups=chip_groups()
    )


def chip_gather(x):
    chips = lax.axis_size("tp") // CORES
    return chip_exchange(jnp.broadcast_to(x, (chips, *x.shape)))


def sibling_swap(x):
    count = lax.axis_size("tp")
    return lax.ppermute(x, "tp", [(source, source ^ 1) for source in range(count)])


def from_sibling(x):
    both = lax.all_gather(x, "tp", axis=0, tiled=False, axis_index_groups=core_groups())
    return jnp.where(lax.axis_index("tp") % CORES == 0, both[1], both[0])


def of_core(blocks, dim, core):
    return lax.dynamic_index_in_dim(blocks, core, dim, keepdims=False)


def product(gathered, weight):
    return lax.dot_general(
        gathered, weight, (((0, 2), (1, 2)), ((), ())), preferred_element_type=jnp.float32
    )


def pair_product(gathered, own, other):
    mine = product(gathered, own)
    theirs = product(gathered, other)
    return mine + from_sibling(theirs)


def attention_grads(upstream, queries, keys, values):
    rows, columns = queries.shape
    heads = columns // HEAD_DIM
    query_grads, key_grads, value_grads = [], [], []

    def dot(a, b, da, db):
        return lax.dot_general(a, b, (((da,), (db,)), ((), ())), preferred_element_type=jnp.float32)

    for head in range(heads):
        cols = slice(head * HEAD_DIM, (head + 1) * HEAD_DIM)
        q, k, v, u = queries[:, cols], keys[:, cols], values[:, cols], upstream[:, cols]
        attention = jax.nn.softmax(dot(q, k, 1, 1), axis=-1)
        weights = attention.astype(jnp.bfloat16)
        output = dot(weights, v, 1, 0)
        delta = jnp.sum(u.astype(jnp.float32) * output, axis=-1, keepdims=True)
        prob_grad = dot(u, v, 1, 1)
        score_grad = (attention * (prob_grad - delta)).astype(jnp.bfloat16)
        query_grads.append(dot(score_grad, k, 1, 0))
        key_grads.append(dot(score_grad, q, 0, 0))
        value_grads.append(dot(weights, u, 0, 0))
    return tuple(
        jnp.concatenate(parts, axis=1).astype(jnp.bfloat16)
        for parts in (query_grads, key_grads, value_grads)
    )


def body(
    grad_in,
    fresh_grads,
    acc_in,
    queries,
    keys,
    values,
    query_weight,
    key_weight,
    value_weight,
    out_weight,
):
    chips = lax.axis_size("tp") // CORES
    core = lax.axis_index("tp") % CORES
    is_top = lax.axis_index("section") == lax.axis_size("section") - 1
    slot_count = queries.shape[1]
    width = queries.shape[3]

    grad_slice = grad_in[0]
    gathered = chip_gather(grad_slice)

    def by_features_last(weight):
        blocks = weight[0].reshape(width, chips, CORES, width)
        own = of_core(blocks, 2, core)
        return own, sibling_swap(of_core(blocks, 2, 1 - core))

    def by_features_first(weight):
        blocks = weight[0].reshape(chips, CORES, width, width)
        own = of_core(blocks, 1, core)
        return own, sibling_swap(of_core(blocks, 1, 1 - core))

    w_out = by_features_last(out_weight)
    w_query = by_features_last(query_weight)
    w_key = by_features_first(key_weight)
    w_value = by_features_first(value_weight)
    w_term = jnp.concatenate([w_key[0], w_value[0], w_key[1], w_value[1]], axis=2)

    def term_parts(key_grad, value_grad):
        own = jnp.concatenate([key_grad, value_grad], axis=1)
        both = jnp.concatenate([own, from_sibling(own)], axis=1)
        parts = jnp.einsum("cfk,rk->crf", w_term, both, preferred_element_type=jnp.float32)
        return parts.astype(jnp.bfloat16)

    carried = acc_in[0]
    passed = grad_slice
    for slot in range(slot_count):
        last = slot + 1 == slot_count
        upstream = pair_product(gathered, *w_out).astype(jnp.bfloat16)
        query_grad, key_grad, value_grad = attention_grads(
            upstream, queries[0, slot], keys[0, slot], values[0, slot]
        )
        if last:
            terms = term_parts(key_grad, value_grad)
            queries_out = jnp.broadcast_to(query_grad, terms.shape)
            arrived = chip_exchange(jnp.stack([queries_out, terms], axis=1))
            all_queries, arrived_terms = arrived[:, 0], arrived[:, 1]
        else:
            all_queries = chip_gather(query_grad)
        branch = pair_product(all_queries, *w_query)
        passed = (grad_slice.astype(jnp.float32) + branch).astype(jnp.bfloat16)
        if not last:
            received = passed_along(passed, "section", -1)
            arrived_terms = chip_exchange(term_parts(key_grad, value_grad))
        carried = carried + arrived_terms.astype(jnp.float32).sum(axis=0)
        if not last:
            carried = passed_along(carried.astype(jnp.bfloat16), "section", -1).astype(jnp.float32)
            grad_slice = jnp.where(is_top, fresh_grads[slot], received)
            gathered = chip_gather(grad_slice)
    return (passed[None], carried[None])


def solution(mesh):
    in_specs = (
        P("section", None, "tp"),
        P(None, None, "tp"),
        P("section", None, "tp"),
        P("section", None, None, "tp"),
        P("section", None, None, "tp"),
        P("section", None, None, "tp"),
        P("section", "tp", None),
        P("section", None, "tp"),
        P("section", None, "tp"),
        P("section", "tp", None),
    )
    out_specs = (P("section", None, "tp"), P("section", None, "tp"))
    return jax.shard_map(body, mesh=mesh, in_specs=in_specs, out_specs=out_specs, check_vma=False)
```

```python
import functools

import jax
import jax.numpy as jnp
from jax import lax
from jax.experimental import pallas as pl
from jax.experimental.pallas import tpu as pltpu
from jax.sharding import PartitionSpec as P

HEAD_DIM = 64
CORES = 2
X = 4
Z = 4
CHIPS = X * Z
W = 128
F32 = jnp.float32
BF16 = jnp.bfloat16
PARAMS = pltpu.CompilerParams(vmem_limit_bytes=24 * 1024 * 1024)


def vmem():
    return pl.BlockSpec(memory_space=pltpu.VMEM)


def anywhere():
    return pl.BlockSpec(memory_space=pl.ANY)


def passed_along(value, axis, steps):
    count = lax.axis_size(axis)
    leading, last = (max(0, -steps), min(count, count - steps))
    return lax.ppermute(value, axis, [(source, source + steps) for source in range(leading, last)])


def member(z, x, core):
    return (z * X + x) * CORES + core


def chip_exchange(parts):
    groups = [[chip * CORES + core for chip in range(CHIPS)] for core in range(CORES)]
    return lax.all_to_all(
        parts, "tp", split_axis=0, concat_axis=0, tiled=True, axis_index_groups=groups
    )


def sibling_swap(value):
    return lax.ppermute(value, "tp", [(i, i ^ 1) for i in range(CHIPS * CORES)])


def core_pair(value):
    groups = [[chip * CORES + core for core in range(CORES)] for chip in range(CHIPS)]
    return lax.all_gather(value, "tp", axis=0, tiled=False, axis_index_groups=groups)


def along_x(value, steps):
    return lax.ppermute(
        value,
        "tp",
        [
            (member(z, x, core), member(z, (x + steps) % X, core))
            for z in range(Z)
            for x in range(X)
            for core in range(CORES)
        ],
    )


def along_z(value, steps):
    return lax.ppermute(
        value,
        "tp",
        [
            (member(z, x, core), member((z + steps) % Z, x, core))
            for z in range(Z)
            for x in range(X)
            for core in range(CORES)
        ],
    )


def dot(a, b, da, db):
    return lax.dot_general(a, b, (((da,), (db,)), ((), ())), preferred_element_type=F32)


def core_index():
    return lax.rem(lax.axis_index("tp"), CORES)


def pack_kernel(wo, wq, wk, wv, oo, oq, ok, ov, so, sq, sk, sv):
    core = core_index()
    for chip in range(CHIPS):
        own = pl.ds(pl.multiple_of((chip * CORES + core) * W, W), W)
        other = pl.ds(pl.multiple_of((chip * CORES + 1 - core) * W, W), W)
        oo[chip] = wo[0, :, own]
        so[chip] = wo[0, :, other]
        oq[chip] = wq[0, :, own]
        sq[chip] = wq[0, :, other]
        ok[chip] = wk[0, own, :]
        sk[chip] = wk[0, other, :]
        ov[chip] = wv[0, own, :]
        sv[chip] = wv[0, other, :]


def pack(wo, wq, wk, wv):
    return pl.pallas_call(
        pack_kernel,
        out_shape=[jax.ShapeDtypeStruct((CHIPS, W, W), BF16)] * 8,
        in_specs=[vmem()] * 4,
        out_specs=[vmem()] * 8,
        compiler_params=PARAMS,
        cost_estimate=pl.CostEstimate(flops=0, bytes_accessed=8 << 20, transcendentals=0),
    )(wo, wq, wk, wv)


def pair_kernel(g, own, other, *rest):
    mine, theirs = rest[-2:]
    total = dot(g[0], other[0], 1, 1)
    for chip in range(1, CHIPS):
        total += dot(g[chip], other[chip], 1, 1)
    theirs[...] = total
    total = dot(g[0], own[0], 1, 1)
    for chip in range(1, CHIPS):
        total += dot(g[chip], own[chip], 1, 1)
    mine[...] = total


def pair_product(gathered, own, other, after=()):
    mine, theirs = pl.pallas_call(
        pair_kernel,
        out_shape=[jax.ShapeDtypeStruct((W, W), F32)] * 2,
        in_specs=[vmem()] * 3 + [anywhere()] * len(after),
        out_specs=[vmem()] * 2,
        compiler_params=PARAMS,
        cost_estimate=pl.CostEstimate(flops=2 * 2 * W * W * W * CHIPS, bytes_accessed=2 << 20, transcendentals=0),
    )(gathered, own, other, *after)
    return mine, core_pair(theirs)


def attention_kernel(slot, mine, both, queries, keys, values, *rest):
    qbc, kv = rest[-2:]
    upstream = (mine[...] + both[1 - core_index()]).astype(BF16)
    q_all, k_all, v_all = queries[0, slot], keys[0, slot], values[0, slot]
    lane = lax.broadcasted_iota(jnp.int32, (W, W), 1)
    zero = jnp.zeros((W, W), BF16)
    query_grad = key_grad = value_grad = None
    for head in range(W // HEAD_DIM):
        inside = (lane // HEAD_DIM) == head
        q = jnp.where(inside, q_all, zero)
        k = jnp.where(inside, k_all, zero)
        u = jnp.where(inside, upstream, zero)
        scores = dot(q, k_all, 1, 1)
        prob_grad = dot(u, v_all, 1, 1)
        top = jnp.max(scores, axis=-1, keepdims=True)
        raised = jnp.exp(scores - top)
        attention = raised / jnp.sum(raised, axis=-1, keepdims=True)
        weights = attention.astype(BF16)
        delta = jnp.sum(weights.astype(F32) * prob_grad, axis=-1, keepdims=True)
        score_grad = (attention * (prob_grad - delta)).astype(BF16)
        parts = (dot(score_grad, k, 1, 0), dot(score_grad, q, 0, 0), dot(weights, u, 0, 0))
        if head == 0:
            query_grad, key_grad, value_grad = parts
        else:
            query_grad, key_grad, value_grad = (
                query_grad + parts[0],
                key_grad + parts[1],
                value_grad + parts[2],
            )
    query_grad = query_grad.astype(BF16)
    for chip in range(CHIPS):
        qbc[chip] = query_grad
    kv[:, :W] = key_grad.astype(BF16)
    kv[:, W:] = value_grad.astype(BF16)


def attention_grads(mine, both, queries, keys, values, slot, after=()):
    return pl.pallas_call(
        functools.partial(attention_kernel, slot),
        out_shape=[
            jax.ShapeDtypeStruct((CHIPS, W, W), BF16),
            jax.ShapeDtypeStruct((W, 2 * W), BF16),
        ],
        in_specs=[vmem()] * 5 + [anywhere()] * len(after),
        out_specs=[vmem()] * 2,
        compiler_params=PARAMS,
        cost_estimate=pl.CostEstimate(flops=20 * W * W * W, bytes_accessed=1 << 20, transcendentals=2 * W * W),
    )(mine, both, queries, keys, values, *after)


def term_kernel(kv, both, ok, ov, rk, rv, *outs):
    own = kv[...]
    other = both[1 - core_index()]
    index = lax.axis_index("tp") // CORES
    z, x = index // X, lax.rem(index, X)
    for step in range(X):
        for j in range(Z):
            chip = lax.rem(z + j, Z) * X + lax.rem(x + step, X)
            total = dot(own[:, :W], ok[chip], 1, 1)
            total += dot(own[:, W:], ov[chip], 1, 1)
            total += dot(other[:, :W], rk[chip], 1, 1)
            total += dot(other[:, W:], rv[chip], 1, 1)
            outs[step][j] = total.astype(BF16)


def term_parts(kv, w_key, w_value):
    return pl.pallas_call(
        term_kernel,
        out_shape=[jax.ShapeDtypeStruct((Z, W, W), BF16)] * X,
        in_specs=[vmem()] * 6,
        out_specs=[vmem()] * X,
        compiler_params=PARAMS,
        cost_estimate=pl.CostEstimate(flops=2 * W * W * 4 * W * CHIPS, bytes_accessed=3 << 20, transcendentals=0),
    )(kv, core_pair(kv), w_key[0], w_value[0], w_key[1], w_value[1])


def spread_kernel(x, *rest):
    out = rest[-1]
    value = x[...].reshape(W, W)
    for chip in range(CHIPS):
        out[chip] = value


def spread(x, after=()):
    return pl.pallas_call(
        spread_kernel,
        out_shape=jax.ShapeDtypeStruct((CHIPS, W, W), BF16),
        in_specs=[vmem()] + [anywhere()] * len(after),
        out_specs=vmem(),
        compiler_params=PARAMS,
    )(x, *after)


def across_x(parts):
    arrived = [parts[0]] + [along_x(parts[step], step) for step in range(1, X)]
    return sum(part.astype(F32) for part in arrived).astype(BF16)


def sum_kernel(start, p0, p1, p2, p3, *rest):
    total = start[...].reshape(W, W)
    for part in (p0, p1, p2, p3):
        total += part[...].astype(F32)
    rest[-1][...] = total


def across_z(start, parts, after=()):
    arrived = [parts[0]] + [along_z(parts[step], step) for step in range(1, Z)]
    return pl.pallas_call(
        sum_kernel,
        out_shape=jax.ShapeDtypeStruct((W, W), F32),
        in_specs=[vmem()] * (1 + Z) + [anywhere()] * len(after),
        out_specs=vmem(),
        compiler_params=PARAMS,
    )(start, *arrived, *after)


def body(
    grad_in,
    fresh_grads,
    acc_in,
    queries,
    keys,
    values,
    query_weight,
    key_weight,
    value_weight,
    out_weight,
):
    is_top = lax.axis_index("section") == lax.axis_size("section") - 1
    is_core_0 = core_index() == 0
    slot_count = queries.shape[1]

    grad_slice = grad_in[0]
    gathered = chip_exchange(spread(grad_in))
    oo, oq, ok, ov, so, sq, sk, sv = pack(out_weight, query_weight, key_weight, value_weight)
    w_out = oo, sibling_swap(so)
    w_query = oq, sibling_swap(sq)
    w_key = ok, sibling_swap(sk)
    w_value = ov, sibling_swap(sv)

    carried = acc_in[0]
    passed = grad_slice
    ready = (w_query[1], w_key[1], w_value[1])
    summed_z = ()
    for slot in range(slot_count):
        last = slot + 1 == slot_count
        mine, both = pair_product(gathered, *w_out, after=ready)
        query_parts, kv = attention_grads(mine, both, queries, keys, values, slot, after=summed_z)
        all_queries = chip_exchange(query_parts)
        parts = term_parts(kv, w_key, w_value)
        mine, both = pair_product(all_queries, *w_query, after=() if last else parts)
        other = jnp.where(is_core_0, both[1], both[0])
        passed = (grad_slice.astype(F32) + mine + other).astype(BF16)
        terms = across_x(parts)
        if not last:
            received = passed_along(passed, "section", -1)
            grad_slice = jnp.where(is_top, fresh_grads[slot], received)
            gathered = chip_exchange(spread(grad_slice, after=(terms,)))
        carried = across_z(carried, terms, after=(both,) if last else ())
        if not last:
            carried = carried.astype(BF16)
            ready = (carried,)
            carried = passed_along(carried, "section", -1)
            summed_z = (carried,)
            carried = carried.astype(F32)
    return (passed[None], carried[None])


def solution(mesh):
    in_specs = (
        P("section", None, "tp"),
        P(None, None, "tp"),
        P("section", None, "tp"),
        P("section", None, None, "tp"),
        P("section", None, None, "tp"),
        P("section", None, None, "tp"),
        P("section", "tp", None),
        P("section", None, "tp"),
        P("section", None, "tp"),
        P("section", "tp", None),
    )
    out_specs = (P("section", None, "tp"), P("section", None, "tp"))
    return jax.shard_map(body, mesh=mesh, in_specs=in_specs, out_specs=out_specs, check_vma=False)
```

```python
import functools

import jax
import jax.numpy as jnp
from jax import lax
from jax.experimental import pallas as pl
from jax.experimental.pallas import tpu as pltpu
from jax.sharding import PartitionSpec as P

HEAD_DIM = 64
CORES = 2
X = 4
Z = 4
CHIPS = X * Z
W = 128
F32 = jnp.float32
BF16 = jnp.bfloat16
PARAMS = pltpu.CompilerParams(vmem_limit_bytes=24 * 1024 * 1024)


def vmem():
    return pl.BlockSpec(memory_space=pltpu.VMEM)


def hbm():
    return pl.BlockSpec(memory_space=pltpu.HBM)


def anywhere():
    return pl.BlockSpec(memory_space=pl.ANY)


def passed_along(value, axis, steps):
    count = lax.axis_size(axis)
    leading, last = (max(0, -steps), min(count, count - steps))
    return lax.ppermute(value, axis, [(source, source + steps) for source in range(leading, last)])


def chip_exchange(parts):
    groups = [[chip * CORES + core for chip in range(CHIPS)] for core in range(CORES)]
    return lax.all_to_all(
        parts, "tp", split_axis=0, concat_axis=0, tiled=True, axis_index_groups=groups
    )


def member(z, x, core):
    return (z * X + x) * CORES + core


def exchange(parts, groups):
    return lax.all_to_all(
        parts, "tp", split_axis=0, concat_axis=0, tiled=True, axis_index_groups=groups
    )


def x_exchange(parts):
    return exchange(
        parts,
        [[member(z, x, core) for x in range(X)] for z in range(Z) for core in range(CORES)],
    )


def z_exchange(parts):
    return exchange(
        parts,
        [[member(z, x, core) for z in range(Z)] for x in range(X) for core in range(CORES)],
    )


def sibling_swap(value):
    return lax.ppermute(value, "tp", [(i, i ^ 1) for i in range(CHIPS * CORES)])


def core_pair(value):
    groups = [[chip * CORES + core for core in range(CORES)] for chip in range(CHIPS)]
    return lax.all_gather(value, "tp", axis=0, tiled=False, axis_index_groups=groups)


def dot(a, b, da, db):
    return lax.dot_general(a, b, (((da,), (db,)), ((), ())), preferred_element_type=F32)


def core_index():
    return lax.rem(lax.axis_index("tp"), CORES)


def halves():
    core = core_index()
    for chip in range(CHIPS):
        own = pl.ds(pl.multiple_of((chip * CORES + core) * W, W), W)
        other = pl.ds(pl.multiple_of((chip * CORES + 1 - core) * W, W), W)
        yield chip, own, other


def pack_columns_kernel(a, b, own_a, own_b, other_a, other_b):
    for chip, own, other in halves():
        other_a[chip] = a[0, :, other]
        other_b[chip] = b[0, :, other]
        own_a[chip] = a[0, :, own]
        own_b[chip] = b[0, :, own]


def pack_rows_kernel(a, b, *rest):
    own_a, own_b, other_a, other_b = rest[-4:]
    for chip, own, other in halves():
        other_a[chip] = a[0, other, :]
        other_b[chip] = b[0, other, :]
        own_a[chip] = a[0, own, :]
        own_b[chip] = b[0, own, :]


def pack(kernel, a, b, after=()):
    own_a, own_b, other_a, other_b = pl.pallas_call(
        kernel,
        out_shape=[jax.ShapeDtypeStruct((CHIPS, W, W), BF16)] * 4,
        in_specs=[vmem()] * 2 + [anywhere()] * len(after),
        out_specs=[vmem()] * 4,
        compiler_params=PARAMS,
        cost_estimate=pl.CostEstimate(flops=0, bytes_accessed=4 << 20, transcendentals=0),
    )(a, b, *after)
    return (own_a, sibling_swap(other_a)), (own_b, sibling_swap(other_b))


def pair_kernel(after, g, own, other, *rest):
    mine, theirs = rest[after:][:2]
    for out, weight in ((theirs, other), (mine, own)):
        out[...] = sum(dot(g[chip], weight[chip], 1, 1) for chip in range(CHIPS))


def last_pair_kernel(arrived, own, other, start, mine, theirs, total):
    for out, weight in ((theirs, other), (mine, own)):
        out[...] = sum(dot(arrived[chip, 0], weight[chip], 1, 1) for chip in range(CHIPS))
    total[...] = start[...].astype(F32) + sum(arrived[chip, 1].astype(F32) for chip in range(CHIPS))


def last_pair_product(arrived, own, other, start):
    mine, theirs, total = pl.pallas_call(
        last_pair_kernel,
        out_shape=[jax.ShapeDtypeStruct((W, W), F32)] * 3,
        in_specs=[vmem()] * 4,
        out_specs=[vmem()] * 3,
        compiler_params=PARAMS,
        cost_estimate=pl.CostEstimate(flops=2 * 2 * W * W * W * CHIPS, bytes_accessed=2 << 20, transcendentals=0),
    )(arrived, own, other, start)
    return mine, core_pair(theirs), total


def pair_product(gathered, own, other, after=(), held=()):
    fixed = 3 + len(after)
    mine, theirs, *freed = pl.pallas_call(
        functools.partial(pair_kernel, len(after + held)),
        out_shape=[jax.ShapeDtypeStruct((W, W), F32)] * 2
        + [jax.ShapeDtypeStruct(x.shape, x.dtype) for x in held],
        in_specs=[vmem()] * 3 + [anywhere()] * len(after + held),
        out_specs=[vmem()] * 2 + [anywhere()] * len(held),
        input_output_aliases={fixed + i: 2 + i for i in range(len(held))},
        compiler_params=PARAMS,
        cost_estimate=pl.CostEstimate(flops=2 * 2 * W * W * W * CHIPS, bytes_accessed=2 << 20, transcendentals=0),
    )(gathered, own, other, *after, *held)
    return mine, core_pair(theirs), *freed


def passed_kernel(grad, mine, both, passed):
    total = grad[...].reshape(W, W).astype(F32) + mine[...] + both[1 - core_index()]
    passed[...] = total.astype(BF16)


def passed_grad(grad, mine, both):
    return pl.pallas_call(
        passed_kernel,
        out_shape=jax.ShapeDtypeStruct((W, W), BF16),
        in_specs=[vmem()] * 3,
        out_specs=vmem(),
        compiler_params=PARAMS,
    )(grad, mine, both)


def send_to_all(value, out, sems):
    copies = [pltpu.make_async_copy(value, out.at[chip], sems.at[chip]) for chip in range(CHIPS)]
    for copy in copies:
        copy.start()
    return copies


def attention_kernel(slot, copied, mine, both, queries, keys, values, out, kv, *scratch):
    upstream = (mine[...] + both[1 - core_index()]).astype(BF16)
    q_all, k_all, v_all = queries[0, slot], keys[0, slot], values[0, slot]
    lane = lax.broadcasted_iota(jnp.int32, (W, W), 1)
    zero = jnp.zeros((W, W), BF16)
    query_grad = jnp.zeros((W, W), F32)
    kept = []
    for head in range(W // HEAD_DIM):
        inside = (lane // HEAD_DIM) == head
        q = jnp.where(inside, q_all, zero)
        k = jnp.where(inside, k_all, zero)
        u = jnp.where(inside, upstream, zero)
        scores = dot(q, k_all, 1, 1)
        prob_grad = dot(u, v_all, 1, 1)
        top = jnp.max(scores, axis=-1, keepdims=True)
        raised = jnp.exp(scores - top)
        attention = raised / jnp.sum(raised, axis=-1, keepdims=True)
        weights = attention.astype(BF16)
        delta = jnp.sum(weights.astype(F32) * prob_grad, axis=-1, keepdims=True)
        score_grad = (attention * (prob_grad - delta)).astype(BF16)
        query_grad += dot(score_grad, k, 1, 0)
        kept.append((score_grad, q, weights, u))
    copies = []
    if copied:
        held, sems = scratch
        held[...] = query_grad.astype(BF16)
        copies = send_to_all(held, out, sems)
    else:
        out[...] = query_grad.astype(BF16)
    key_grad = sum(dot(score_grad, q, 0, 0) for score_grad, q, _, _ in kept)
    value_grad = sum(dot(weights, u, 0, 0) for _, _, weights, u in kept)
    kv[:, :W] = key_grad.astype(BF16)
    kv[:, W:] = value_grad.astype(BF16)
    for copy in copies:
        copy.wait()


def attention_grads(mine, both, queries, keys, values, slot, copied):
    return pl.pallas_call(
        functools.partial(attention_kernel, slot, copied),
        out_shape=[
            pltpu.HBM((CHIPS, W, W), BF16) if copied else jax.ShapeDtypeStruct((W, W), BF16),
            jax.ShapeDtypeStruct((W, 2 * W), BF16),
        ],
        in_specs=[vmem()] * 5,
        out_specs=[hbm() if copied else vmem(), vmem()],
        scratch_shapes=[pltpu.VMEM((W, W), BF16), pltpu.SemaphoreType.DMA((CHIPS,))] if copied else [],
        compiler_params=PARAMS,
        cost_estimate=pl.CostEstimate(flops=20 * W * W * W, bytes_accessed=1 << 20, transcendentals=2 * W * W),
    )(mine, both, queries, keys, values)


def term_of(chip, own, other, ok, ov, rk, rv):
    total = dot(own[:, :W], ok[chip], 1, 1)
    total += dot(own[:, W:], ov[chip], 1, 1)
    total += dot(other[:, :W], rk[chip], 1, 1)
    total += dot(other[:, W:], rv[chip], 1, 1)
    return total.astype(BF16)


def term_kernel(kv, both, ok, ov, rk, rv, out):
    own, other = kv[...], both[1 - core_index()]
    for chip in range(CHIPS):
        out[chip % X, chip // X] = term_of(chip, own, other, ok, ov, rk, rv)


def last_kernel(kv, both, query_grad, ok, ov, rk, rv, *rest):
    out, held, term_sems, query_sems = rest[-4:]
    copies = [
        pltpu.make_async_copy(query_grad, out.at[chip, 0], query_sems.at[chip])
        for chip in range(CHIPS)
    ]
    for copy in copies:
        copy.start()
    own, other = kv[...], both[1 - core_index()]
    for chip in range(CHIPS):
        held[chip] = term_of(chip, own, other, ok, ov, rk, rv)
        copies.append(pltpu.make_async_copy(held.at[chip], out.at[chip, 1], term_sems.at[chip]))
        copies[-1].start()
    for copy in copies:
        copy.wait()


TERM_COST = pl.CostEstimate(flops=2 * W * W * 4 * W * CHIPS, bytes_accessed=3 << 20, transcendentals=0)


def term_parts(kv, w_key, w_value):
    return pl.pallas_call(
        term_kernel,
        out_shape=jax.ShapeDtypeStruct((X, Z, W, W), BF16),
        in_specs=[vmem()] * 6,
        out_specs=vmem(),
        compiler_params=PARAMS,
        cost_estimate=TERM_COST,
    )(kv, core_pair(kv), w_key[0], w_value[0], w_key[1], w_value[1])


def last_parts(kv, query_grad, w_key, w_value, after):
    return pl.pallas_call(
        last_kernel,
        out_shape=pltpu.HBM((CHIPS, 2, W, W), BF16),
        in_specs=[vmem()] * 7 + [anywhere()] * len(after),
        out_specs=hbm(),
        scratch_shapes=[
            pltpu.VMEM((CHIPS, W, W), BF16),
            pltpu.SemaphoreType.DMA((CHIPS,)),
            pltpu.SemaphoreType.DMA((CHIPS,)),
        ],
        compiler_params=PARAMS,
        cost_estimate=TERM_COST,
    )(kv, core_pair(kv), query_grad, w_key[0], w_value[0], w_key[1], w_value[1], *after)


def x_sum_kernel(parts, out):
    for z in range(Z):
        out[z] = sum(parts[x, z].astype(F32) for x in range(X)).astype(BF16)


def x_sum(parts):
    return pl.pallas_call(
        x_sum_kernel,
        out_shape=jax.ShapeDtypeStruct((Z, W, W), BF16),
        in_specs=[vmem()],
        out_specs=vmem(),
        compiler_params=PARAMS,
    )(parts)


def z_sum_kernel(start, parts, out):
    total = start[0] + sum(parts[z].astype(F32) for z in range(Z))
    out[...] = total.astype(BF16)


def z_sum(start, parts):
    return pl.pallas_call(
        z_sum_kernel,
        out_shape=jax.ShapeDtypeStruct((W, W), BF16),
        in_specs=[vmem()] * 2,
        out_specs=vmem(),
        compiler_params=PARAMS,
    )(start, parts)


def spread_kernel(x, *rest):
    out, sems = rest[-2:]
    for copy in send_to_all(x, out, sems):
        copy.wait()


def spread(x, after=()):
    return pl.pallas_call(
        spread_kernel,
        out_shape=pltpu.HBM((CHIPS, W, W), BF16),
        in_specs=[anywhere()] * (1 + len(after)),
        out_specs=hbm(),
        scratch_shapes=[pltpu.SemaphoreType.DMA((CHIPS,))],
        compiler_params=PARAMS,
    )(x, *after)


def next_kernel(slot, received, fresh, chosen):
    top = lax.axis_size("section") - 1
    chosen[...] = jnp.where(lax.axis_index("section") == top, fresh[slot], received[...])


def next_grad(received, fresh, slot):
    return pl.pallas_call(
        functools.partial(next_kernel, slot),
        out_shape=jax.ShapeDtypeStruct((W, W), BF16),
        in_specs=[vmem()] * 2,
        out_specs=vmem(),
        compiler_params=PARAMS,
        cost_estimate=pl.CostEstimate(flops=40_000_000_000, bytes_accessed=1 << 17, transcendentals=0),
    )(received, fresh)


def body(
    grad_in,
    fresh_grads,
    acc_in,
    queries,
    keys,
    values,
    query_weight,
    key_weight,
    value_weight,
    out_weight,
):
    slot_count = queries.shape[1]

    grad_slice = grad_in[0]
    gathered = chip_exchange(spread(grad_slice))
    w_out, w_query = pack(pack_columns_kernel, out_weight, query_weight)
    ready = (w_query[1],)
    passed = grad_slice
    for slot in range(slot_count):
        last = slot + 1 == slot_count
        mine, both = pair_product(gathered, *w_out, after=() if slot else ready)
        query_grad, kv = attention_grads(mine, both, queries, keys, values, slot, copied=not last)
        if slot == 0:
            w_key, w_value = pack(pack_rows_kernel, key_weight, value_weight, after=(mine,))
        if last:
            arrived = chip_exchange(last_parts(kv, query_grad, w_key, w_value, ready))
            mine, both, carried = last_pair_product(arrived, *w_query, carried)
        else:
            all_queries = chip_exchange(query_grad)
            terms = term_parts(kv, w_key, w_value)
            mine, both, terms = pair_product(all_queries, *w_query, held=(terms,))
        passed = passed_grad(grad_slice, mine, both)
        if not last:
            received = passed_along(passed, "section", -1)
            along_z = z_exchange(x_sum(x_exchange(terms)))
            grad_slice = next_grad(received, fresh_grads, slot)
            gathered = chip_exchange(spread(grad_slice, after=(along_z,)))
            carried = passed_along(z_sum(acc_in, along_z), "section", -1)
            ready = (carried,)
    return (passed[None], carried[None])


def solution(mesh):
    in_specs = (
        P("section", None, "tp"),
        P(None, None, "tp"),
        P("section", None, "tp"),
        P("section", None, None, "tp"),
        P("section", None, None, "tp"),
        P("section", None, None, "tp"),
        P("section", "tp", None),
        P("section", None, "tp"),
        P("section", None, "tp"),
        P("section", "tp", None),
    )
    out_specs = (P("section", None, "tp"), P("section", None, "tp"))
    return jax.shard_map(body, mesh=mesh, in_specs=in_specs, out_specs=out_specs, check_vma=False)
```

```python
import functools

import jax
import jax.numpy as jnp
from jax import lax
from jax.experimental import pallas as pl
from jax.experimental.pallas import tpu as pltpu
from jax.sharding import PartitionSpec as P

HEAD_DIM = 64
CORES = 2
X = 4
Z = 4
CHIPS = X * Z
Z_HI = 4
W = 128
F32 = jnp.float32
BF16 = jnp.bfloat16
PARAMS = pltpu.CompilerParams(vmem_limit_bytes=24 * 1024 * 1024)


def vmem():
    return pl.BlockSpec(memory_space=pltpu.VMEM)


def hbm():
    return pl.BlockSpec(memory_space=pltpu.HBM)


def anywhere():
    return pl.BlockSpec(memory_space=pl.ANY)


def below(value, sources):
    return lax.ppermute(value, "section", [(source, source - 1) for source in sources])


def chip_exchange(parts):
    groups = [[chip * CORES + core for chip in range(CHIPS)] for core in range(CORES)]
    return lax.all_to_all(
        parts, "tp", split_axis=0, concat_axis=0, tiled=True, axis_index_groups=groups
    )


def member(z, x, core):
    return (z * X + x) * CORES + core


def exchange(parts, groups):
    return lax.all_to_all(
        parts, "tp", split_axis=0, concat_axis=0, tiled=True, axis_index_groups=groups
    )


def x_exchange(parts):
    return exchange(
        parts,
        [[member(z, x, core) for x in range(X)] for z in range(Z) for core in range(CORES)],
    )


def along(value, x_steps, z_steps):
    return lax.ppermute(
        value,
        "tp",
        [
            (member(z, x, core), member((z + z_steps) % Z, (x + x_steps) % X, core))
            for z in range(Z)
            for x in range(X)
            for core in range(CORES)
        ],
    )


def place():
    chip = lax.axis_index("tp") // CORES
    return chip // X, lax.rem(chip, X)


def sibling_swap(value):
    return lax.ppermute(value, "tp", [(i, i ^ 1) for i in range(CHIPS * CORES)])


def core_pair(value):
    groups = [[chip * CORES + core for core in range(CORES)] for chip in range(CHIPS)]
    return lax.all_gather(value, "tp", axis=0, tiled=False, axis_index_groups=groups)


def dot(a, b, da, db):
    return lax.dot_general(a, b, (((da,), (db,)), ((), ())), preferred_element_type=F32)


def core_index():
    return lax.rem(lax.axis_index("tp"), CORES)


def halves():
    core = core_index()
    for chip in range(CHIPS):
        own = pl.ds(pl.multiple_of((chip * CORES + core) * W, W), W)
        other = pl.ds(pl.multiple_of((chip * CORES + 1 - core) * W, W), W)
        yield chip, own, other


def pack_columns_kernel(a, b, own_a, own_b, other_a, other_b):
    for chip, own, other in halves():
        other_a[chip] = a[0, :, other]
        other_b[chip] = b[0, :, other]
        own_a[chip] = a[0, :, own]
        own_b[chip] = b[0, :, own]


def pack_rows_kernel(a, b, *rest):
    own_a, own_b, other_a, other_b = rest[-4:]
    for chip, own, other in halves():
        other_a[chip] = a[0, other, :]
        other_b[chip] = b[0, other, :]
        own_a[chip] = a[0, own, :]
        own_b[chip] = b[0, own, :]


def pack(kernel, a, b, after=()):
    own_a, own_b, other_a, other_b = pl.pallas_call(
        kernel,
        out_shape=[jax.ShapeDtypeStruct((CHIPS, W, W), BF16)] * 4,
        in_specs=[vmem()] * 2 + [anywhere()] * len(after),
        out_specs=[vmem()] * 4,
        compiler_params=PARAMS,
        cost_estimate=pl.CostEstimate(flops=0, bytes_accessed=4 << 20, transcendentals=0),
    )(a, b, *after)
    return (own_a, sibling_swap(other_a)), (own_b, sibling_swap(other_b))


def pair_kernel(after, g, own, other, *rest):
    mine, theirs = rest[after:][:2]
    for out, weight in ((theirs, other), (mine, own)):
        out[...] = sum(dot(g[chip], weight[chip], 1, 1) for chip in range(CHIPS))


def last_pair_kernel(arrived, own, other, near, far, mine, theirs, total):
    for out, weight in ((theirs, other), (mine, own)):
        out[...] = sum(dot(arrived[chip, 0], weight[chip], 1, 1) for chip in range(CHIPS))
    total[...] = near[...] + far[...].astype(F32) + sum(arrived[chip, 1].astype(F32) for chip in range(CHIPS))


def last_pair_product(arrived, own, other, near, far):
    mine, theirs, total = pl.pallas_call(
        last_pair_kernel,
        out_shape=[jax.ShapeDtypeStruct((W, W), F32)] * 3,
        in_specs=[vmem()] * 5,
        out_specs=[vmem()] * 3,
        compiler_params=PARAMS,
        cost_estimate=pl.CostEstimate(flops=2 * 2 * W * W * W * CHIPS, bytes_accessed=2 << 20, transcendentals=0),
    )(arrived, own, other, near, far)
    return mine, core_pair(theirs), total


def pair_product(gathered, own, other, after=()):
    mine, theirs = pl.pallas_call(
        functools.partial(pair_kernel, len(after)),
        out_shape=[jax.ShapeDtypeStruct((W, W), F32)] * 2,
        in_specs=[vmem()] * 3 + [anywhere()] * len(after),
        out_specs=[vmem()] * 2,
        compiler_params=PARAMS,
        cost_estimate=pl.CostEstimate(flops=2 * 2 * W * W * W * CHIPS, bytes_accessed=2 << 20, transcendentals=0),
    )(gathered, own, other, *after)
    return mine, core_pair(theirs)


def passed_kernel(count, grad, mine, both, *rest):
    total = grad[...].reshape(W, W).astype(F32) + mine[...] + both[1 - core_index()]
    rest[count][...] = total.astype(BF16)


def passed_grad(grad, mine, both, held=()):
    return pl.pallas_call(
        functools.partial(passed_kernel, len(held)),
        out_shape=[jax.ShapeDtypeStruct((W, W), BF16)]
        + [jax.ShapeDtypeStruct(x.shape, x.dtype) for x in held],
        in_specs=[vmem()] * 3 + [anywhere()] * len(held),
        out_specs=[vmem()] + [anywhere()] * len(held),
        input_output_aliases={3 + i: 1 + i for i in range(len(held))},
        compiler_params=PARAMS,
    )(grad, mine, both, *held)


def send_to_all(value, out, sems):
    copies = [pltpu.make_async_copy(value, out.at[chip], sems.at[chip]) for chip in range(CHIPS)]
    for copy in copies:
        copy.start()
    return copies


def attention_kernel(slot, copied, mine, both, queries, keys, values, out, kv, *scratch):
    upstream = (mine[...] + both[1 - core_index()]).astype(BF16)
    q_all, k_all, v_all = queries[0, slot], keys[0, slot], values[0, slot]
    lane = lax.broadcasted_iota(jnp.int32, (W, W), 1)
    zero = jnp.zeros((W, W), BF16)
    query_grad = jnp.zeros((W, W), F32)
    kept = []
    for head in range(W // HEAD_DIM):
        inside = (lane // HEAD_DIM) == head
        q = jnp.where(inside, q_all, zero)
        k = jnp.where(inside, k_all, zero)
        u = jnp.where(inside, upstream, zero)
        scores = dot(q, k_all, 1, 1)
        prob_grad = dot(u, v_all, 1, 1)
        top = jnp.max(scores, axis=-1, keepdims=True)
        raised = jnp.exp(scores - top)
        attention = raised / jnp.sum(raised, axis=-1, keepdims=True)
        weights = attention.astype(BF16)
        delta = jnp.sum(weights.astype(F32) * prob_grad, axis=-1, keepdims=True)
        score_grad = (attention * (prob_grad - delta)).astype(BF16)
        query_grad += dot(score_grad, k, 1, 0)
        kept.append((score_grad, q, weights, u))
    copies = []
    if copied:
        held, sems = scratch
        held[...] = query_grad.astype(BF16)
        copies = send_to_all(held, out, sems)
    else:
        out[...] = query_grad.astype(BF16)
    key_grad = sum(dot(score_grad, q, 0, 0) for score_grad, q, _, _ in kept)
    value_grad = sum(dot(weights, u, 0, 0) for _, _, weights, u in kept)
    kv[:, :W] = key_grad.astype(BF16)
    kv[:, W:] = value_grad.astype(BF16)
    for copy in copies:
        copy.wait()


def attention_grads(mine, both, queries, keys, values, slot, copied):
    return pl.pallas_call(
        functools.partial(attention_kernel, slot, copied),
        out_shape=[
            pltpu.HBM((CHIPS, W, W), BF16) if copied else jax.ShapeDtypeStruct((W, W), BF16),
            jax.ShapeDtypeStruct((W, 2 * W), BF16),
        ],
        in_specs=[vmem()] * 5,
        out_specs=[hbm() if copied else vmem(), vmem()],
        scratch_shapes=[pltpu.VMEM((W, W), BF16), pltpu.SemaphoreType.DMA((CHIPS,))] if copied else [],
        compiler_params=PARAMS,
        cost_estimate=pl.CostEstimate(flops=20 * W * W * W, bytes_accessed=1 << 20, transcendentals=2 * W * W),
    )(mine, both, queries, keys, values)


def term_of(chip, own, other, ok, ov, rk, rv):
    total = dot(own[:, :W], ok[chip], 1, 1)
    total += dot(own[:, W:], ov[chip], 1, 1)
    total += dot(other[:, :W], rk[chip], 1, 1)
    total += dot(other[:, W:], rv[chip], 1, 1)
    return total.astype(BF16)


def term_kernel(kv, both, ok, ov, rk, rv, out):
    own, other = kv[...], both[1 - core_index()]
    for chip in range(CHIPS):
        out[chip % X, chip // X] = term_of(chip, own, other, ok, ov, rk, rv)


def last_kernel(kv, both, query_grad, ok, ov, rk, rv, *rest):
    out, held, term_sems, query_sems = rest[-4:]
    copies = [
        pltpu.make_async_copy(query_grad, out.at[chip, 0], query_sems.at[chip])
        for chip in range(CHIPS)
    ]
    for copy in copies:
        copy.start()
    own, other = kv[...], both[1 - core_index()]
    for chip in range(CHIPS):
        held[chip] = term_of(chip, own, other, ok, ov, rk, rv)
        copies.append(pltpu.make_async_copy(held.at[chip], out.at[chip, 1], term_sems.at[chip]))
        copies[-1].start()
    for copy in copies:
        copy.wait()


TERM_COST = pl.CostEstimate(flops=2 * W * W * 4 * W * CHIPS, bytes_accessed=3 << 20, transcendentals=0)


def term_parts(kv, w_key, w_value):
    return pl.pallas_call(
        term_kernel,
        out_shape=jax.ShapeDtypeStruct((X, Z, W, W), BF16),
        in_specs=[vmem()] * 6,
        out_specs=vmem(),
        compiler_params=PARAMS,
        cost_estimate=TERM_COST,
    )(kv, core_pair(kv), w_key[0], w_value[0], w_key[1], w_value[1])


def last_parts(kv, query_grad, w_key, w_value, after):
    return pl.pallas_call(
        last_kernel,
        out_shape=pltpu.HBM((CHIPS, 2, W, W), BF16),
        in_specs=[vmem()] * 7 + [anywhere()] * len(after),
        out_specs=hbm(),
        scratch_shapes=[
            pltpu.VMEM((CHIPS, W, W), BF16),
            pltpu.SemaphoreType.DMA((CHIPS,)),
            pltpu.SemaphoreType.DMA((CHIPS,)),
        ],
        compiler_params=PARAMS,
        cost_estimate=TERM_COST,
    )(kv, core_pair(kv), query_grad, w_key[0], w_value[0], w_key[1], w_value[1], *after)


def x_sum_kernel(parts, *outs):
    z, _ = place()
    for step, out in enumerate(outs):
        to_z = lax.rem(z + step, Z)
        out[...] = sum(parts[x, to_z].astype(F32) for x in range(X)).astype(BF16)


def x_sum(parts):
    return pl.pallas_call(
        x_sum_kernel,
        out_shape=[jax.ShapeDtypeStruct((W, W), BF16)] * Z,
        in_specs=[vmem()],
        out_specs=[vmem()] * Z,
        compiler_params=PARAMS,
    )(parts)


def z_sum_kernel(start, *rest):
    rest[-1][...] = (start[0] + sum(part[...].astype(F32) for part in rest[:-1])).astype(BF16)


def z_sum(start, parts):
    return pl.pallas_call(
        z_sum_kernel,
        out_shape=jax.ShapeDtypeStruct((W, W), BF16),
        in_specs=[vmem()] * (1 + Z),
        out_specs=vmem(),
        compiler_params=PARAMS,
    )(start, *parts)


def landed_kernel(received, *rest):
    rest[-1][...] = received[...].astype(F32)


def landed(received, after):
    return pl.pallas_call(
        landed_kernel,
        out_shape=jax.ShapeDtypeStruct((W, W), F32),
        in_specs=[vmem()] + [anywhere()] * len(after),
        out_specs=vmem(),
        compiler_params=PARAMS,
    )(received, *after)


def spread_kernel(count, x, *rest):
    out, sems = rest[count], rest[-1]
    for copy in send_to_all(x, out, sems):
        copy.wait()


def spread(x, held=()):
    return pl.pallas_call(
        functools.partial(spread_kernel, len(held)),
        out_shape=[pltpu.HBM((CHIPS, W, W), BF16)] + [jax.ShapeDtypeStruct(h.shape, h.dtype) for h in held],
        in_specs=[anywhere()] * (1 + len(held)),
        out_specs=[hbm()] + [anywhere()] * len(held),
        input_output_aliases={1 + i: 1 + i for i in range(len(held))},
        scratch_shapes=[pltpu.SemaphoreType.DMA((CHIPS,))],
        compiler_params=PARAMS,
    )(x, *held)


def next_kernel(slot, received, fresh, chosen):
    top = lax.axis_size("section") - 1
    chosen[...] = jnp.where(lax.axis_index("section") == top, fresh[slot], received[...])


def next_grad(received, fresh, slot):
    return pl.pallas_call(
        functools.partial(next_kernel, slot),
        out_shape=jax.ShapeDtypeStruct((W, W), BF16),
        in_specs=[vmem()] * 2,
        out_specs=vmem(),
        compiler_params=PARAMS,
    )(received, fresh)


def body(
    grad_in,
    fresh_grads,
    acc_in,
    queries,
    keys,
    values,
    query_weight,
    key_weight,
    value_weight,
    out_weight,
):
    slot_count = queries.shape[1]
    sections = lax.axis_size("section")

    grad_slice = grad_in[0]
    gathered = chip_exchange(spread(grad_slice)[0])
    w_out, w_query = pack(pack_columns_kernel, out_weight, query_weight)
    ready = (w_query[1],)
    passed = grad_slice
    for slot in range(slot_count):
        last = slot + 1 == slot_count
        mine, both = pair_product(gathered, *w_out, after=ready)
        query_grad, kv = attention_grads(mine, both, queries, keys, values, slot, copied=not last)
        if slot == 0:
            w_key, w_value = pack(pack_rows_kernel, key_weight, value_weight, after=(mine,))
        if last:
            near = landed(near, after=(kv,))
            arrived = chip_exchange(last_parts(kv, query_grad, w_key, w_value, (near,)))
            mine, both, carried = last_pair_product(arrived, *w_query, near, far)
        else:
            all_queries = chip_exchange(query_grad)
            terms = term_parts(kv, w_key, w_value)
            mine, both = pair_product(all_queries, *w_query, after=(terms,))
        passed, *terms = passed_grad(grad_slice, mine, both, held=() if last else (terms,))
        if not last:
            received = below(passed, range(1, sections))
            parts = x_sum(x_exchange(*terms))
            grad_slice = next_grad(received, fresh_grads, slot)
            copies, *parts = spread(grad_slice, held=parts)
            gathered = chip_exchange(copies)
            moved = [parts[0]] + [along(parts[step], 0, step) for step in range(1, Z)]
            summed = z_sum(acc_in, moved)
            near = below(summed, [i for i in range(1, sections) if i % Z_HI])
            far = below(summed, range(Z_HI, sections, Z_HI))
            ready = (summed,)
    return (passed[None], carried[None])


def solution(mesh):
    in_specs = (
        P("section", None, "tp"),
        P(None, None, "tp"),
        P("section", None, "tp"),
        P("section", None, None, "tp"),
        P("section", None, None, "tp"),
        P("section", None, None, "tp"),
        P("section", "tp", None),
        P("section", None, "tp"),
        P("section", None, "tp"),
        P("section", "tp", None),
    )
    out_specs = (P("section", None, "tp"), P("section", None, "tp"))
    return jax.shard_map(body, mesh=mesh, in_specs=in_specs, out_specs=out_specs, check_vma=False)
```

```python
import functools

import jax
import jax.numpy as jnp
from jax import lax
from jax.experimental import pallas as pl
from jax.experimental.pallas import tpu as pltpu
from jax.sharding import PartitionSpec as P

HEAD_DIM = 64
CORES = 2
X = 4
Z = 4
CHIPS = X * Z
Z_HI = 4
W = 128
F32 = jnp.float32
BF16 = jnp.bfloat16
PARAMS = pltpu.CompilerParams(vmem_limit_bytes=12 * 1024 * 1024)


def vmem():
    return pl.BlockSpec(memory_space=pltpu.VMEM)


def hbm():
    return pl.BlockSpec(memory_space=pltpu.HBM)


def in_hbm(x):
    return pltpu.with_memory_space_constraint(x, pltpu.HBM)


def anywhere():
    return pl.BlockSpec(memory_space=pl.ANY)


def below(value, sources):
    return lax.ppermute(value, "section", [(source, source - 1) for source in sources])


def chip_exchange(parts):
    groups = [[chip * CORES + core for chip in range(CHIPS)] for core in range(CORES)]
    return lax.all_to_all(
        parts, "tp", split_axis=0, concat_axis=0, tiled=True, axis_index_groups=groups
    )


def member(z, x, core):
    return (z * X + x) * CORES + core


def exchange(parts, groups):
    return lax.all_to_all(
        parts, "tp", split_axis=0, concat_axis=0, tiled=True, axis_index_groups=groups
    )


def x_exchange(parts):
    return exchange(
        parts,
        [[member(z, x, core) for x in range(X)] for z in range(Z) for core in range(CORES)],
    )


def along(value, x_steps, z_steps):
    return lax.ppermute(
        value,
        "tp",
        [
            (member(z, x, core), member((z + z_steps) % Z, (x + x_steps) % X, core))
            for z in range(Z)
            for x in range(X)
            for core in range(CORES)
        ],
    )


def place():
    chip = lax.axis_index("tp") // CORES
    return chip // X, lax.rem(chip, X)


def sibling_swap(value):
    return lax.ppermute(value, "tp", [(i, i ^ 1) for i in range(CHIPS * CORES)])


def core_pair(value):
    groups = [[chip * CORES + core for core in range(CORES)] for chip in range(CHIPS)]
    return lax.all_gather(value, "tp", axis=0, tiled=False, axis_index_groups=groups)


def dot(a, b, da, db):
    return lax.dot_general(a, b, (((da,), (db,)), ((), ())), preferred_element_type=F32)


def core_index():
    return lax.rem(lax.axis_index("tp"), CORES)


def halves():
    core = core_index()
    for chip in range(CHIPS):
        own = pl.ds(pl.multiple_of((chip * CORES + core) * W, W), W)
        other = pl.ds(pl.multiple_of((chip * CORES + 1 - core) * W, W), W)
        yield chip, own, other


def pack_columns_kernel(a, b, grad, own_a, own_b, other_a, other_b, grad_out):
    for chip, own, other in halves():
        there = slice(chip * W, (chip + 1) * W)
        other_a[:, there] = a[0, :, other]
        other_b[:, there] = b[0, :, other]
        own_a[:, there] = a[0, :, own]
        own_b[:, there] = b[0, :, own]
    grad_out[...] = grad[0]


def pack_columns(a, b, grad):
    own_a, own_b, other_a, other_b, grad = pl.pallas_call(
        pack_columns_kernel,
        out_shape=[jax.ShapeDtypeStruct((W, CHIPS * W), BF16)] * 4 + [jax.ShapeDtypeStruct((W, W), BF16)],
        in_specs=[vmem()] * 3,
        out_specs=[vmem()] * 5,
        compiler_params=PARAMS,
        cost_estimate=pl.CostEstimate(flops=0, bytes_accessed=4 << 20, transcendentals=0),
    )(a, b, grad)
    return (own_a, sibling_swap(other_a)), (own_b, sibling_swap(other_b)), grad


def pack_rows_kernel(a, b, *rest):
    own_ab, other_ab = rest[-2:]
    for chip, own, other in halves():
        other_ab[chip, :, :W] = a[0, other, :]
        other_ab[chip, :, W:] = b[0, other, :]
        own_ab[chip, :, :W] = a[0, own, :]
        own_ab[chip, :, W:] = b[0, own, :]


def pack_rows(a, b, after):
    own, other = pl.pallas_call(
        pack_rows_kernel,
        out_shape=[jax.ShapeDtypeStruct((CHIPS, W, 2 * W), BF16)] * 2,
        in_specs=[vmem()] * 2 + [anywhere()] * len(after),
        out_specs=[vmem()] * 2,
        compiler_params=PARAMS,
        cost_estimate=pl.CostEstimate(flops=0, bytes_accessed=4 << 20, transcendentals=0),
    )(a, b, *after)
    return own, sibling_swap(other)


def pair_kernel(after, g, own, other, *rest):
    mine, theirs, joined = rest[after:]
    for chip in range(CHIPS):
        joined[:, chip * W : (chip + 1) * W] = g[chip]
    theirs[...] = dot(joined[...], other[...], 1, 1)
    mine[...] = dot(joined[...], own[...], 1, 1)


def last_pair_kernel(arrived, own, other, near, far, mine, theirs, total, joined):
    for chip in range(CHIPS):
        joined[:, chip * W : (chip + 1) * W] = arrived[chip, 0]
    theirs[...] = dot(joined[...], other[...], 1, 1)
    mine[...] = dot(joined[...], own[...], 1, 1)
    total[...] = near[...] + far[...].astype(F32) + sum(arrived[chip, 1].astype(F32) for chip in range(CHIPS))


def last_pair_product(arrived, own, other, near, far):
    mine, theirs, total = pl.pallas_call(
        last_pair_kernel,
        out_shape=[jax.ShapeDtypeStruct((W, W), F32)] * 3,
        in_specs=[vmem()] * 5,
        out_specs=[vmem()] * 3,
        scratch_shapes=[pltpu.VMEM((W, CHIPS * W), BF16)],
        compiler_params=PARAMS,
        cost_estimate=pl.CostEstimate(flops=2 * 2 * W * W * W * CHIPS, bytes_accessed=2 << 20, transcendentals=0),
    )(arrived, own, other, near, far)
    return mine, core_pair(theirs), total


def pair_product(gathered, own, other, after=()):
    mine, theirs = pl.pallas_call(
        functools.partial(pair_kernel, len(after)),
        out_shape=[jax.ShapeDtypeStruct((W, W), F32)] * 2,
        in_specs=[vmem()] * 3 + [anywhere()] * len(after),
        out_specs=[vmem()] * 2,
        scratch_shapes=[pltpu.VMEM((W, CHIPS * W), BF16)],
        compiler_params=PARAMS,
        cost_estimate=pl.CostEstimate(flops=2 * 2 * W * W * W * CHIPS, bytes_accessed=2 << 20, transcendentals=0),
    )(gathered, own, other, *after)
    return mine, core_pair(theirs)


def passed_kernel(count, grad, mine, both, *rest):
    total = grad[...].reshape(W, W).astype(F32) + mine[...] + both[1 - core_index()]
    rest[count][...] = total.astype(BF16)


def passed_grad(grad, mine, both, held=()):
    return pl.pallas_call(
        functools.partial(passed_kernel, len(held)),
        out_shape=[jax.ShapeDtypeStruct((W, W), BF16)]
        + [jax.ShapeDtypeStruct(x.shape, x.dtype) for x in held],
        in_specs=[vmem()] * 3 + [anywhere()] * len(held),
        out_specs=[vmem()] + [anywhere()] * len(held),
        input_output_aliases={3 + i: 1 + i for i in range(len(held))},
        compiler_params=PARAMS,
    )(grad, mine, both, *held)


def send_to_all(value, out, sems):
    copies = [pltpu.make_async_copy(value, out.at[chip], sems.at[chip]) for chip in range(CHIPS)]
    for copy in copies:
        copy.start()
    return copies


def attention_kernel(slot, copied, mine, both, queries, keys, values, out, kv, *scratch):
    upstream = (mine[...] + both[1 - core_index()]).astype(BF16)
    q_all, k_all, v_all = queries[0, slot], keys[0, slot], values[0, slot]
    lane = lax.broadcasted_iota(jnp.int32, (W, W), 1)
    zero = jnp.zeros((W, W), BF16)
    query_grad = jnp.zeros((W, W), F32)
    kept = []
    for head in range(W // HEAD_DIM):
        inside = (lane // HEAD_DIM) == head
        q = jnp.where(inside, q_all, zero)
        k = jnp.where(inside, k_all, zero)
        u = jnp.where(inside, upstream, zero)
        scores = dot(q, k_all, 1, 1)
        prob_grad = dot(u, v_all, 1, 1)
        top = jnp.max(scores, axis=-1, keepdims=True)
        raised = jnp.exp(scores - top)
        attention = raised / jnp.sum(raised, axis=-1, keepdims=True)
        weights = attention.astype(BF16)
        delta = jnp.sum(weights.astype(F32) * prob_grad, axis=-1, keepdims=True)
        score_grad = (attention * (prob_grad - delta)).astype(BF16)
        query_grad += dot(score_grad, k, 1, 0)
        kept.append((score_grad, q, weights, u))
    copies = []
    if copied:
        held, sems = scratch
        held[...] = query_grad.astype(BF16)
        copies = send_to_all(held, out, sems)
    else:
        out[...] = query_grad.astype(BF16)
    key_grad = sum(dot(score_grad, q, 0, 0) for score_grad, q, _, _ in kept)
    value_grad = sum(dot(weights, u, 0, 0) for _, _, weights, u in kept)
    kv[:, :W] = key_grad.astype(BF16)
    kv[:, W:] = value_grad.astype(BF16)
    for copy in copies:
        copy.wait()


def attention_grads(mine, both, queries, keys, values, slot, copied):
    return pl.pallas_call(
        functools.partial(attention_kernel, slot, copied),
        out_shape=[
            pltpu.HBM((CHIPS, W, W), BF16) if copied else jax.ShapeDtypeStruct((W, W), BF16),
            jax.ShapeDtypeStruct((W, 2 * W), BF16),
        ],
        in_specs=[vmem()] * 5,
        out_specs=[hbm() if copied else vmem(), vmem()],
        scratch_shapes=[pltpu.VMEM((W, W), BF16), pltpu.SemaphoreType.DMA((CHIPS,))] if copied else [],
        compiler_params=PARAMS,
        cost_estimate=pl.CostEstimate(flops=20 * W * W * W, bytes_accessed=1 << 20, transcendentals=2 * W * W),
    )(mine, both, queries, keys, values)


def term_of(chip, own, other, own_weight, other_weight):
    return (dot(own, own_weight[chip], 1, 1) + dot(other, other_weight[chip], 1, 1)).astype(BF16)


def term_kernel(kv, both, own_weight, other_weight, out):
    own, other = kv[...], both[1 - core_index()]
    for chip in range(CHIPS):
        out[chip % X, chip // X] = term_of(chip, own, other, own_weight, other_weight)


def last_kernel(kv, both, query_grad, own_weight, other_weight, *rest):
    out, held, term_sems, query_sems = rest[-4:]
    copies = [
        pltpu.make_async_copy(query_grad, out.at[chip, 0], query_sems.at[chip])
        for chip in range(CHIPS)
    ]
    for copy in copies:
        copy.start()
    own, other = kv[...], both[1 - core_index()]
    for chip in range(CHIPS):
        held[chip] = term_of(chip, own, other, own_weight, other_weight)
        copies.append(pltpu.make_async_copy(held.at[chip], out.at[chip, 1], term_sems.at[chip]))
        copies[-1].start()
    for copy in copies:
        copy.wait()


TERM_COST = pl.CostEstimate(flops=2 * W * W * 4 * W * CHIPS, bytes_accessed=3 << 20, transcendentals=0)


def term_parts(kv, w_term):
    return pl.pallas_call(
        term_kernel,
        out_shape=jax.ShapeDtypeStruct((X, Z, W, W), BF16),
        in_specs=[vmem()] * 4,
        out_specs=vmem(),
        compiler_params=PARAMS,
        cost_estimate=TERM_COST,
    )(kv, core_pair(kv), *w_term)


def last_parts(kv, query_grad, w_term, after):
    return pl.pallas_call(
        last_kernel,
        out_shape=pltpu.HBM((CHIPS, 2, W, W), BF16),
        in_specs=[vmem()] * 5 + [anywhere()] * len(after),
        out_specs=hbm(),
        scratch_shapes=[
            pltpu.VMEM((CHIPS, W, W), BF16),
            pltpu.SemaphoreType.DMA((CHIPS,)),
            pltpu.SemaphoreType.DMA((CHIPS,)),
        ],
        compiler_params=PARAMS,
        cost_estimate=TERM_COST,
    )(kv, core_pair(kv), query_grad, *w_term, *after)


def x_sum_kernel(parts, *rest):
    z, _ = place()
    for step, out in enumerate(rest[-Z:]):
        to_z = lax.rem(z + step, Z)
        out[...] = sum(parts[x, to_z].astype(F32) for x in range(X)).astype(BF16)


def x_sum(parts, after):
    return pl.pallas_call(
        x_sum_kernel,
        out_shape=[jax.ShapeDtypeStruct((W, W), BF16)] * Z,
        in_specs=[vmem()] + [hbm()] * len(after),
        out_specs=[vmem()] * Z,
        compiler_params=PARAMS,
    )(parts, *after)


def z_sum_kernel(start, *rest):
    rest[-1][...] = (start[0] + sum(part[...].astype(F32) for part in rest[:-1])).astype(BF16)


def z_sum(start, parts):
    return pl.pallas_call(
        z_sum_kernel,
        out_shape=jax.ShapeDtypeStruct((W, W), BF16),
        in_specs=[vmem()] * (1 + Z),
        out_specs=vmem(),
        compiler_params=PARAMS,
    )(start, *parts)


def landed_kernel(received, *rest):
    rest[-1][...] = received[...].astype(F32)


def landed(received, after):
    return pl.pallas_call(
        landed_kernel,
        out_shape=jax.ShapeDtypeStruct((W, W), F32),
        in_specs=[vmem()] + [anywhere()] * len(after),
        out_specs=vmem(),
        compiler_params=PARAMS,
    )(received, *after)


def spread_kernel(x, *rest):
    out, sems = rest[-2:]
    for copy in send_to_all(x.at[0] if len(x.shape) == 3 else x, out, sems):
        copy.wait()


def spread(x, source, after=()):
    return pl.pallas_call(
        spread_kernel,
        out_shape=pltpu.HBM((CHIPS, W, W), BF16),
        in_specs=[source] + [anywhere()] * len(after),
        out_specs=hbm(),
        scratch_shapes=[pltpu.SemaphoreType.DMA((CHIPS,))],
        compiler_params=PARAMS,
    )(x, *after)


def next_kernel(slot, received, fresh, chosen):
    top = lax.axis_size("section") - 1
    chosen[...] = jnp.where(lax.axis_index("section") == top, fresh[slot], received[...])


def next_grad(received, fresh, slot):
    return pl.pallas_call(
        functools.partial(next_kernel, slot),
        out_shape=jax.ShapeDtypeStruct((W, W), BF16),
        in_specs=[vmem()] * 2,
        out_specs=vmem(),
        compiler_params=PARAMS,
    )(received, fresh)


def body(
    grad_in,
    fresh_grads,
    acc_in,
    queries,
    keys,
    values,
    query_weight,
    key_weight,
    value_weight,
    out_weight,
):
    slot_count = queries.shape[1]
    sections = lax.axis_size("section")

    gathered = chip_exchange(spread(grad_in, hbm()))
    w_out, w_query, grad_slice = pack_columns(out_weight, query_weight, grad_in)
    ready = (w_query[1],)
    for slot in range(slot_count):
        last = slot + 1 == slot_count
        mine, both = pair_product(gathered, *w_out, after=ready)
        query_grad, kv = attention_grads(mine, both, queries, keys, values, slot, copied=not last)
        if slot == 0:
            w_term = pack_rows(key_weight, value_weight, after=(mine,))
        if last:
            near = landed(near, after=(kv,))
            arrived = chip_exchange(last_parts(kv, query_grad, w_term, (near,)))
            mine, both, carried = last_pair_product(arrived, *w_query, near, far)
        else:
            all_queries = chip_exchange(query_grad)
            terms = term_parts(kv, w_term)
            mine, both = pair_product(all_queries, *w_query, after=(terms,))
        passed, *terms = passed_grad(grad_slice, mine, both, held=() if last else (terms,))
        if not last:
            received = below(passed, range(1, sections))
            arrived = x_exchange(*terms)
            grad_slice = next_grad(received, fresh_grads, slot)
            copies = spread(grad_slice, vmem(), after=(arrived,))
            gathered = chip_exchange(copies)
            parts = x_sum(arrived, after=(in_hbm(copies),))
            moved = [parts[0]] + [along(parts[step], 0, step) for step in range(1, Z)]
            summed = z_sum(acc_in, moved)
            near = below(summed, [i for i in range(1, sections) if i % Z_HI])
            far = below(summed, range(Z_HI, sections, Z_HI))
            ready = (summed,)
    return (passed[None], carried[None])


def solution(mesh):
    in_specs = (
        P("section", None, "tp"),
        P(None, None, "tp"),
        P("section", None, "tp"),
        P("section", None, None, "tp"),
        P("section", None, None, "tp"),
        P("section", None, None, "tp"),
        P("section", "tp", None),
        P("section", None, "tp"),
        P("section", None, "tp"),
        P("section", "tp", None),
    )
    out_specs = (P("section", None, "tp"), P("section", None, "tp"))
    return jax.shard_map(body, mesh=mesh, in_specs=in_specs, out_specs=out_specs, check_vma=False)
```

```python
import functools

import jax
import jax.numpy as jnp
from jax import lax
from jax.experimental import pallas as pl
from jax.experimental.pallas import tpu as pltpu
from jax.sharding import PartitionSpec as P

HEAD_DIM = 64
CORES = 2
X = 4
Z = 4
CHIPS = X * Z
Z_HI = 4
W = 128
F32 = jnp.float32
BF16 = jnp.bfloat16
PARAMS = pltpu.CompilerParams(vmem_limit_bytes=12 * 1024 * 1024)


def vmem():
    return pl.BlockSpec(memory_space=pltpu.VMEM)


def hbm():
    return pl.BlockSpec(memory_space=pltpu.HBM)


def in_hbm(x):
    return pltpu.with_memory_space_constraint(x, pltpu.HBM)


def anywhere():
    return pl.BlockSpec(memory_space=pl.ANY)


def below(value, sources):
    return lax.ppermute(value, "section", [(source, source - 1) for source in sources])


def chip_exchange(parts):
    groups = [[chip * CORES + core for chip in range(CHIPS)] for core in range(CORES)]
    return lax.all_to_all(
        parts, "tp", split_axis=0, concat_axis=0, tiled=True, axis_index_groups=groups
    )


def member(z, x, core):
    return (z * X + x) * CORES + core


def exchange(parts, groups):
    return lax.all_to_all(
        parts, "tp", split_axis=0, concat_axis=0, tiled=True, axis_index_groups=groups
    )


def x_exchange(parts):
    return exchange(
        parts,
        [[member(z, x, core) for x in range(X)] for z in range(Z) for core in range(CORES)],
    )


def along(value, x_steps, z_steps):
    return lax.ppermute(
        value,
        "tp",
        [
            (member(z, x, core), member((z + z_steps) % Z, (x + x_steps) % X, core))
            for z in range(Z)
            for x in range(X)
            for core in range(CORES)
        ],
    )


def place():
    chip = lax.axis_index("tp") // CORES
    return chip // X, lax.rem(chip, X)


def sibling_swap(value):
    return lax.ppermute(value, "tp", [(i, i ^ 1) for i in range(CHIPS * CORES)])


def core_pair(value):
    groups = [[chip * CORES + core for core in range(CORES)] for chip in range(CHIPS)]
    return lax.all_gather(value, "tp", axis=0, tiled=False, axis_index_groups=groups)


def dot(a, b, da, db):
    return lax.dot_general(a, b, (((da,), (db,)), ((), ())), preferred_element_type=F32)


def core_index():
    return lax.rem(lax.axis_index("tp"), CORES)


def halves():
    core = core_index()
    for chip in range(CHIPS):
        own = pl.ds(pl.multiple_of((chip * CORES + core) * W, W), W)
        other = pl.ds(pl.multiple_of((chip * CORES + 1 - core) * W, W), W)
        yield chip, own, other


def pack_columns_kernel(a, b, grad, own_a, own_b, other_a, other_b, grad_out):
    for chip, own, other in halves():
        there = slice(chip * W, (chip + 1) * W)
        other_a[:, there] = a[0, :, other]
        other_b[:, there] = b[0, :, other]
        own_a[:, there] = a[0, :, own]
        own_b[:, there] = b[0, :, own]
    grad_out[...] = grad[0]


def pack_columns(a, b, grad):
    own_a, own_b, other_a, other_b, grad = pl.pallas_call(
        pack_columns_kernel,
        out_shape=[jax.ShapeDtypeStruct((W, CHIPS * W), BF16)] * 4 + [jax.ShapeDtypeStruct((W, W), BF16)],
        in_specs=[vmem()] * 3,
        out_specs=[vmem()] * 5,
        compiler_params=PARAMS,
        cost_estimate=pl.CostEstimate(flops=0, bytes_accessed=4 << 20, transcendentals=0),
    )(a, b, grad)
    return (own_a, sibling_swap(other_a)), (own_b, sibling_swap(other_b)), grad


def pack_rows_kernel(a, b, *rest):
    own_a, own_b, other_a, other_b = rest[-4:]
    for chip, own, other in halves():
        other_a[chip] = a[0, other, :]
        other_b[chip] = b[0, other, :]
        own_a[chip] = a[0, own, :]
        own_b[chip] = b[0, own, :]


def pack_rows(a, b, after):
    own_a, own_b, other_a, other_b = pl.pallas_call(
        pack_rows_kernel,
        out_shape=[jax.ShapeDtypeStruct((CHIPS, W, W), BF16)] * 4,
        in_specs=[vmem()] * 2 + [anywhere()] * len(after),
        out_specs=[vmem()] * 4,
        compiler_params=PARAMS,
        cost_estimate=pl.CostEstimate(flops=0, bytes_accessed=4 << 20, transcendentals=0),
    )(a, b, *after)
    return own_a, own_b, sibling_swap(other_a), sibling_swap(other_b)


def pair_kernel(after, g, own, other, *rest):
    mine, theirs, joined = rest[after:]
    for chip in range(CHIPS):
        joined[:, chip * W : (chip + 1) * W] = g[chip]
    theirs[...] = dot(joined[...], other[...], 1, 1)
    mine[...] = dot(joined[...], own[...], 1, 1)


def last_pair_kernel(arrived, own, other, near, far, mine, theirs, total, joined):
    for chip in range(CHIPS):
        joined[:, chip * W : (chip + 1) * W] = arrived[chip, 0]
    theirs[...] = dot(joined[...], other[...], 1, 1)
    mine[...] = dot(joined[...], own[...], 1, 1)
    total[...] = near[...] + far[...].astype(F32) + sum(arrived[chip, 1].astype(F32) for chip in range(CHIPS))


def last_pair_product(arrived, own, other, near, far):
    mine, theirs, total = pl.pallas_call(
        last_pair_kernel,
        out_shape=[jax.ShapeDtypeStruct((W, W), F32)] * 3,
        in_specs=[vmem()] * 5,
        out_specs=[vmem()] * 3,
        scratch_shapes=[pltpu.VMEM((W, CHIPS * W), BF16)],
        compiler_params=PARAMS,
        cost_estimate=pl.CostEstimate(flops=2 * 2 * W * W * W * CHIPS, bytes_accessed=2 << 20, transcendentals=0),
    )(arrived, own, other, near, far)
    return mine, core_pair(theirs), total


def pair_product(gathered, own, other, after=()):
    mine, theirs = pl.pallas_call(
        functools.partial(pair_kernel, len(after)),
        out_shape=[jax.ShapeDtypeStruct((W, W), F32)] * 2,
        in_specs=[vmem()] * 3 + [anywhere()] * len(after),
        out_specs=[vmem()] * 2,
        scratch_shapes=[pltpu.VMEM((W, CHIPS * W), BF16)],
        compiler_params=PARAMS,
        cost_estimate=pl.CostEstimate(flops=2 * 2 * W * W * W * CHIPS, bytes_accessed=2 << 20, transcendentals=0),
    )(gathered, own, other, *after)
    return mine, core_pair(theirs)


def passed_kernel(count, grad, mine, both, *rest):
    total = grad[...].reshape(W, W).astype(F32) + mine[...] + both[1 - core_index()]
    rest[count][...] = total.astype(BF16)


def passed_grad(grad, mine, both, held=()):
    return pl.pallas_call(
        functools.partial(passed_kernel, len(held)),
        out_shape=[jax.ShapeDtypeStruct((W, W), BF16)]
        + [jax.ShapeDtypeStruct(x.shape, x.dtype) for x in held],
        in_specs=[vmem()] * 3 + [anywhere()] * len(held),
        out_specs=[vmem()] + [anywhere()] * len(held),
        input_output_aliases={3 + i: 1 + i for i in range(len(held))},
        compiler_params=PARAMS,
    )(grad, mine, both, *held)


def send_to_all(value, out, sems):
    copies = [pltpu.make_async_copy(value, out.at[chip], sems.at[chip]) for chip in range(CHIPS)]
    for copy in copies:
        copy.start()
    return copies


def attention_kernel(slot, copied, mine, both, queries, keys, values, out, kv, *scratch):
    upstream = (mine[...] + both[1 - core_index()]).astype(BF16)
    q_all, k_all, v_all = queries[0, slot], keys[0, slot], values[0, slot]
    lane = lax.broadcasted_iota(jnp.int32, (W, W), 1)
    zero = jnp.zeros((W, W), BF16)
    query_grad = jnp.zeros((W, W), F32)
    kept = []
    for head in range(W // HEAD_DIM):
        inside = (lane // HEAD_DIM) == head
        q = jnp.where(inside, q_all, zero)
        k = jnp.where(inside, k_all, zero)
        u = jnp.where(inside, upstream, zero)
        scores = dot(q, k_all, 1, 1)
        prob_grad = dot(u, v_all, 1, 1)
        top = jnp.max(scores, axis=-1, keepdims=True)
        raised = jnp.exp(scores - top)
        attention = raised / jnp.sum(raised, axis=-1, keepdims=True)
        weights = attention.astype(BF16)
        delta = jnp.sum(weights.astype(F32) * prob_grad, axis=-1, keepdims=True)
        score_grad = (attention * (prob_grad - delta)).astype(BF16)
        query_grad += dot(score_grad, k, 1, 0)
        kept.append((score_grad, q, weights, u))
    copies = []
    if copied:
        held, sems = scratch
        held[...] = query_grad.astype(BF16)
        copies = send_to_all(held, out, sems)
    else:
        out[...] = query_grad.astype(BF16)
    key_grad = sum(dot(score_grad, q, 0, 0) for score_grad, q, _, _ in kept)
    value_grad = sum(dot(weights, u, 0, 0) for _, _, weights, u in kept)
    kv[:, :W] = key_grad.astype(BF16)
    kv[:, W:] = value_grad.astype(BF16)
    for copy in copies:
        copy.wait()


def attention_grads(mine, both, queries, keys, values, slot, copied):
    return pl.pallas_call(
        functools.partial(attention_kernel, slot, copied),
        out_shape=[
            pltpu.HBM((CHIPS, W, W), BF16) if copied else jax.ShapeDtypeStruct((W, W), BF16),
            jax.ShapeDtypeStruct((W, 2 * W), BF16),
        ],
        in_specs=[vmem()] * 5,
        out_specs=[hbm() if copied else vmem(), vmem()],
        scratch_shapes=[pltpu.VMEM((W, W), BF16), pltpu.SemaphoreType.DMA((CHIPS,))] if copied else [],
        compiler_params=PARAMS,
        cost_estimate=pl.CostEstimate(flops=20 * W * W * W, bytes_accessed=1 << 20, transcendentals=2 * W * W),
    )(mine, both, queries, keys, values)


def term_of(chip, own, other, ok, ov, rk, rv):
    total = dot(own[:, :W], ok[chip], 1, 1)
    total += dot(own[:, W:], ov[chip], 1, 1)
    total += dot(other[:, :W], rk[chip], 1, 1)
    total += dot(other[:, W:], rv[chip], 1, 1)
    return total.astype(BF16)


def term_kernel(kv, both, ok, ov, rk, rv, out):
    own, other = kv[...], both[1 - core_index()]
    for chip in range(CHIPS):
        out[chip % X, chip // X] = term_of(chip, own, other, ok, ov, rk, rv)


def last_kernel(kv, both, query_grad, ok, ov, rk, rv, *rest):
    out, held, term_sems, query_sems = rest[-4:]
    copies = [
        pltpu.make_async_copy(query_grad, out.at[chip, 0], query_sems.at[chip])
        for chip in range(CHIPS)
    ]
    for copy in copies:
        copy.start()
    own, other = kv[...], both[1 - core_index()]
    for chip in range(CHIPS):
        held[chip] = term_of(chip, own, other, ok, ov, rk, rv)
        copies.append(pltpu.make_async_copy(held.at[chip], out.at[chip, 1], term_sems.at[chip]))
        copies[-1].start()
    for copy in copies:
        copy.wait()


TERM_COST = pl.CostEstimate(flops=2 * W * W * 4 * W * CHIPS, bytes_accessed=3 << 20, transcendentals=0)


def term_parts(kv, w_term):
    return pl.pallas_call(
        term_kernel,
        out_shape=jax.ShapeDtypeStruct((X, Z, W, W), BF16),
        in_specs=[vmem()] * 6,
        out_specs=vmem(),
        compiler_params=PARAMS,
        cost_estimate=TERM_COST,
    )(kv, core_pair(kv), *w_term)


def last_parts(kv, query_grad, w_term, after):
    return pl.pallas_call(
        last_kernel,
        out_shape=pltpu.HBM((CHIPS, 2, W, W), BF16),
        in_specs=[vmem()] * 7 + [anywhere()] * len(after),
        out_specs=hbm(),
        scratch_shapes=[
            pltpu.VMEM((CHIPS, W, W), BF16),
            pltpu.SemaphoreType.DMA((CHIPS,)),
            pltpu.SemaphoreType.DMA((CHIPS,)),
        ],
        compiler_params=PARAMS,
        cost_estimate=TERM_COST,
    )(kv, core_pair(kv), query_grad, *w_term, *after)


def x_sum_kernel(parts, *rest):
    z, _ = place()
    for step, out in enumerate(rest[-Z:]):
        to_z = lax.rem(z + step, Z)
        out[...] = sum(parts[x, to_z].astype(F32) for x in range(X)).astype(BF16)


def x_sum(parts, after):
    return pl.pallas_call(
        x_sum_kernel,
        out_shape=[jax.ShapeDtypeStruct((W, W), BF16)] * Z,
        in_specs=[vmem()] + [hbm()] * len(after),
        out_specs=[vmem()] * Z,
        compiler_params=PARAMS,
    )(parts, *after)


def z_sum_kernel(start, *rest):
    rest[-1][...] = (start[0] + sum(part[...].astype(F32) for part in rest[:-1])).astype(BF16)


def z_sum(start, parts):
    return pl.pallas_call(
        z_sum_kernel,
        out_shape=jax.ShapeDtypeStruct((W, W), BF16),
        in_specs=[vmem()] * (1 + Z),
        out_specs=vmem(),
        compiler_params=PARAMS,
    )(start, *parts)


def landed_kernel(received, *rest):
    rest[-1][...] = received[...].astype(F32)


def landed(received, after):
    return pl.pallas_call(
        landed_kernel,
        out_shape=jax.ShapeDtypeStruct((W, W), F32),
        in_specs=[vmem()] + [anywhere()] * len(after),
        out_specs=vmem(),
        compiler_params=PARAMS,
    )(received, *after)


def spread_kernel(x, *rest):
    out, sems = rest[-2:]
    for copy in send_to_all(x.at[0] if len(x.shape) == 3 else x, out, sems):
        copy.wait()


def spread(x, source, after=()):
    return pl.pallas_call(
        spread_kernel,
        out_shape=pltpu.HBM((CHIPS, W, W), BF16),
        in_specs=[source] + [anywhere()] * len(after),
        out_specs=hbm(),
        scratch_shapes=[pltpu.SemaphoreType.DMA((CHIPS,))],
        compiler_params=PARAMS,
    )(x, *after)


def next_kernel(slot, received, fresh, chosen):
    top = lax.axis_size("section") - 1
    chosen[...] = jnp.where(lax.axis_index("section") == top, fresh[slot], received[...])


def next_grad(received, fresh, slot):
    return pl.pallas_call(
        functools.partial(next_kernel, slot),
        out_shape=jax.ShapeDtypeStruct((W, W), BF16),
        in_specs=[vmem()] * 2,
        out_specs=vmem(),
        compiler_params=PARAMS,
    )(received, fresh)


def body(
    grad_in,
    fresh_grads,
    acc_in,
    queries,
    keys,
    values,
    query_weight,
    key_weight,
    value_weight,
    out_weight,
):
    slot_count = queries.shape[1]
    sections = lax.axis_size("section")

    gathered = chip_exchange(spread(grad_in, hbm()))
    w_out, w_query, grad_slice = pack_columns(out_weight, query_weight, grad_in)
    ready = (w_query[1],)
    for slot in range(slot_count):
        last = slot + 1 == slot_count
        mine, both = pair_product(gathered, *w_out, after=ready)
        query_grad, kv = attention_grads(mine, both, queries, keys, values, slot, copied=not last)
        if slot == 0:
            w_term = pack_rows(key_weight, value_weight, after=(mine,))
        if last:
            near = landed(near, after=(kv,))
            arrived = chip_exchange(last_parts(kv, query_grad, w_term, (near,)))
            mine, both, carried = last_pair_product(arrived, *w_query, near, far)
        else:
            all_queries = chip_exchange(query_grad)
            terms = term_parts(kv, w_term)
            mine, both = pair_product(all_queries, *w_query, after=(terms,))
        passed, *terms = passed_grad(grad_slice, mine, both, held=() if last else (terms,))
        if not last:
            received = below(passed, range(1, sections))
            arrived = x_exchange(*terms)
            grad_slice = next_grad(received, fresh_grads, slot)
            copies = spread(grad_slice, vmem(), after=(arrived,))
            gathered = chip_exchange(copies)
            parts = x_sum(arrived, after=(in_hbm(copies),))
            moved = [parts[0]] + [along(parts[step], 0, step) for step in range(1, Z)]
            summed = z_sum(acc_in, moved)
            near = below(summed, [i for i in range(1, sections) if i % Z_HI])
            far = below(summed, range(Z_HI, sections, Z_HI))
            ready = (summed,)
    return (passed[None], carried[None])


def solution(mesh):
    in_specs = (
        P("section", None, "tp"),
        P(None, None, "tp"),
        P("section", None, "tp"),
        P("section", None, None, "tp"),
        P("section", None, None, "tp"),
        P("section", None, None, "tp"),
        P("section", "tp", None),
        P("section", None, "tp"),
        P("section", None, "tp"),
        P("section", "tp", None),
    )
    out_specs = (P("section", None, "tp"), P("section", None, "tp"))
    return jax.shard_map(body, mesh=mesh, in_specs=in_specs, out_specs=out_specs, check_vma=False)
```
